32 devices in a mesh: groups: 2 (over x), owner: 2 (over core), tensor: 8 (over z, y).
Axes of the slice: x: 2, y: 2, z: 4, core: 2. Of those that a mesh axis runs over, the one named last changes fastest.
Arguments:
- hidden: bfloat16 [3072, 8192], P(('groups', 'owner'), 'tensor'), parts along dimension 0, may hold values from -6 to 6
- channel_smooth_scale: float32 [8192], P('tensor'), may hold values from 0.3 to 3
- weight: bfloat16 [8192, 8192], P('tensor'), may hold values from -0.09375 to 0.09375
- shrink_matrix_bank: bfloat16 [128, 64, 8192], P(('groups', 'owner'), None, 'tensor'), parts along dimension 0, may hold values from -0.0625 to 0.0625
- expand_matrix_bank: bfloat16 [128, 64, 8192], P(('groups', 'owner'), None, 'tensor'), parts along dimension 0, may hold values from -0.75 to 0.75
- row_adapter_index: int32 [3072, 1], P(('groups', 'owner')), parts along dimension 0, may hold values from 0 to 63; in each aligned block of 768 rows (0 to 767, 768 to 1535, ...) at most 30 rows name the same one
- adapter_storage_slot: int32 [128], P('groups'), parts along dimension 0, may hold values from 0 to 63, each once
Outputs:
- output: bfloat16 [3072, 8192], P(('groups', 'owner'), 'tensor'), parts along dimension 0
The draws below stay inside these ranges and needn't reach their ends.
There are 2 independent parts, one for each index of `groups`. The reference program is written for one: setup_inputs(seed, part) draws one part's arguments, and reference() takes and returns one part's arrays. A program takes and returns all parts, laid end to end along the dimension named above; an argument that names none is the same for every part. Nothing has to cross between parts.
Inputs may be any that keep to these rules, and one draw needn't show every extreme that they name: `row_adapter_index`: among the rows of one owner index (aligned blocks of 768 rows) no adapter is named by more than 30 rows, a bound that some block reaches. `adapter_storage_slot`: A permutation: every storage slot holds one adapter.
All inputs are finite; a program needn't handle non-finite values.
Results may differ from the reference program's by a relative error of at most 0.0049.
Values may be sent and summed in bfloat16 or wider, within the bound.
No kernel may reach another device: no remote copies, remote signals or barrier semaphores. Data moves between devices by JAX's collectives and lax.ppermute only.
A program may use at most 192 MiB of HBM per device.

```python
import math
import jax
import jax.numpy as jnp
import numpy as np

MODEL_WIDTH = 8192
ADAPTER_RANK = 64
ROWS_DEV = 768
ADAPTER_TOTAL = 64
ROWS = 1536
SEG = 30


def with_spikes(entries, key, source, target, blocks, factor):
    owner, partner = [(jnp.arange(entries.shape[dim]) // (entries.shape[dim] // blocks)).reshape([-1 if axis == dim else 1 for axis in range(entries.ndim)]) for dim in (source, target)]
    chosen = jax.random.permutation(key, blocks)[partner]
    strong = (owner == chosen) | (owner == (partner + blocks // 2) % blocks)
    return jnp.where(strong, factor * entries, entries)


def level_of(stream_key, extent, cuts, least, high):
    def one(position, blocks):
        heights = jax.random.uniform(jax.random.fold_in(jax.random.fold_in(stream_key, 6), position), (blocks,), jnp.float32, least / len(cuts), high / len(cuts))
        return jnp.repeat(jnp.exp(heights), extent[position] // blocks).reshape((-1,) + (1,) * (len(extent) - position - 1))

    gain = one(*cuts[0])
    for cut in cuts[1:]:
        gain = gain * one(*cut)
    return gain


def routed_block(key, own, number, rows, count, top, reach, slope):
    sequence = jax.random.permutation(key, count)
    packed, ordinary = portions_of(count, rows * top, reach, slope, True), portions_of(count, rows * top, reach, slope, False)
    places = jnp.arange(count)

    def named(lengths, offset_by):
        used = int((lengths > 0).sum())
        fixed = max(1, used // 4)
        shifted = fixed + (places - fixed + offset_by * (used - fixed)) % max(1, count - fixed)
        return jnp.zeros((count,), jnp.int32).at[sequence[jnp.where(places < fixed, places, shifted)]].set(jnp.asarray(lengths, jnp.int32))

    lengths = jnp.where(number % 4 == 0, named(packed, number // 4), named(ordinary, number - number // 4 - 1))
    mixed = jax.random.permutation(jax.random.fold_in(own, 3), count)
    donor, taker = mixed[0:count // 2 * 2:2], mixed[1:count // 2 * 2:2]
    margin = jnp.minimum(lengths[donor] - 1, reach - lengths[taker]) // 2
    margin = jnp.where((donor == sequence[0]) | (taker == sequence[0]) | (lengths[taker] == 0), 0, jnp.maximum(margin, 0))
    shifted = jax.random.randint(jax.random.fold_in(own, 4), (count // 2,), 0, 1 << 20) % (margin + 1)
    lengths = lengths.at[donor].add(-shifted).at[taker].add(shifted)
    members = jnp.searchsorted(jnp.cumsum(lengths), jnp.arange(rows * top), side="right").astype(jnp.int32)
    listing = members.reshape(top, rows).T
    listing = listing[jax.random.permutation(jax.random.fold_in(own, 1), rows)]
    offset_by = jax.random.randint(jax.random.fold_in(own, 2), (rows, 1), 0, top)
    return jnp.take_along_axis(listing, (jnp.arange(top)[None, :] + offset_by) % top, axis=1)


def portions_of(number_of, total, most, skew, full):
    loads = [(1 << 20) // math.isqrt(standing ** skew) + 1 for standing in range(1, number_of + 1)]
    largest = most if full else min(most, max(-(-total // number_of), total * loads[0] // sum(loads)))
    least = 1 if total - largest >= number_of - 1 else 0
    holding, rest = [largest] + [least] * (number_of - 1), total - largest - least * (number_of - 1)
    while rest > 0:
        movable = [i for i in range(1, number_of) if holding[i] < largest] or [i for i in range(1, number_of) if holding[i] < most]
        whole, budget = sum([loads[i] for i in movable]), rest
        for i in movable:
            more = min(most - holding[i], max(1, budget * loads[i] // whole), rest)
            holding[i] = holding[i] + more
            rest = rest - more
    return np.array(holding)


def normal_values(own_key, shape, scale, limit, shards=(), kind=jnp.bfloat16):
    drawn = scale * jax.random.normal(own_key, shape, jnp.float32)
    if shards:
        drawn = drawn * level_of(own_key, shape, shards, -0.22, 0.18)
    return jnp.clip(drawn, -limit, limit).astype(kind)


def bell_draw_with(rng, dims, spread, bound, shards, heavy, held_as=jnp.bfloat16):
    array = spread * jax.random.normal(rng, dims, jnp.float32)
    if shards:
        array = array * level_of(rng, dims, shards, -0.22, 0.18)
    return jnp.clip(with_spikes(array, jax.random.fold_in(rng, 3), *heavy), -bound, bound).astype(held_as)


def setup_inputs(seed: int = 0, part: int = 0) -> dict:
    arg_keys = jax.random.split(jax.random.key(seed), 8)
    part_keys = jax.random.split(jax.random.fold_in(arg_keys[7], part), 8)
    hidden = normal_values(part_keys[0], (ROWS, MODEL_WIDTH), 1.0, 6.0, ((0, 2), (1, 8)))
    channel_smooth_scale = jnp.clip(jnp.exp(math.log(3.0) - 2.3025851 * jax.random.uniform(arg_keys[1], (MODEL_WIDTH,), jnp.float32) ** level_of(arg_keys[1], (MODEL_WIDTH,), ((0, 8),), -0.2, 0.2)), 0.3, 3.0)
    weight = bell_draw_with(arg_keys[2], (MODEL_WIDTH, MODEL_WIDTH), MODEL_WIDTH ** -0.5, 0.09375, ((0, 8),), (0, 1, 8, 2.0))
    shrink_matrix_bank = normal_values(part_keys[3], (ADAPTER_TOTAL, ADAPTER_RANK, MODEL_WIDTH), MODEL_WIDTH ** -0.5, 0.0625, ((0, 2), (2, 8)))
    expand_matrix_bank = normal_values(part_keys[4], (ADAPTER_TOTAL, ADAPTER_RANK, MODEL_WIDTH), ADAPTER_RANK ** -0.5, 0.75, ((0, 2), (2, 8)))
    row_adapter_index_keys = jax.random.split(jax.random.fold_in(part_keys[5], 1), ROWS // ROWS_DEV)
    row_adapter_index_turns = jax.random.permutation(jax.random.fold_in(part_keys[5], 3), ROWS // ROWS_DEV)
    row_adapter_index = jax.vmap(lambda own, number: routed_block(jax.random.fold_in(part_keys[5], 2), own, number, ROWS_DEV, ADAPTER_TOTAL, 1, SEG, 2))(row_adapter_index_keys, row_adapter_index_turns).reshape((ROWS, 1))
    adapter_storage_slot = jax.random.permutation(part_keys[6], ADAPTER_TOTAL).astype(jnp.int32)
    return dict(hidden=hidden, channel_smooth_scale=channel_smooth_scale, weight=weight, shrink_matrix_bank=shrink_matrix_bank, expand_matrix_bank=expand_matrix_bank, row_adapter_index=row_adapter_index, adapter_storage_slot=adapter_storage_slot)


def reference(hidden, channel_smooth_scale, weight, shrink_matrix_bank, expand_matrix_bank, row_adapter_index, adapter_storage_slot):
    smoothed = (hidden.astype(jnp.float32) / channel_smooth_scale).astype(jnp.bfloat16)
    base = jnp.dot(smoothed, weight, preferred_element_type=jnp.float32)
    slot_of = adapter_storage_slot[row_adapter_index[:, 0]]
    column_ids = jnp.arange(ADAPTER_TOTAL, dtype=jnp.int32)
    picked = (slot_of[:, None] == column_ids[None, :]).astype(jnp.float32)
    shrunk_rows_gathered = jnp.dot(hidden, shrink_matrix_bank.reshape(ADAPTER_TOTAL * ADAPTER_RANK, MODEL_WIDTH).T, preferred_element_type=jnp.float32)
    shrunk_rows_gathered = shrunk_rows_gathered.reshape(ROWS, ADAPTER_TOTAL, ADAPTER_RANK)
    shrunk = jnp.sum(shrunk_rows_gathered * picked[:, :, None], axis=1).astype(jnp.bfloat16)
    spread_rows_out = (picked[:, :, None] * shrunk.astype(jnp.float32)[:, None, :]).reshape(ROWS, ADAPTER_TOTAL * ADAPTER_RANK).astype(jnp.bfloat16)
    row_deltas = jnp.dot(spread_rows_out, expand_matrix_bank.reshape(ADAPTER_TOTAL * ADAPTER_RANK, MODEL_WIDTH), preferred_element_type=jnp.float32).astype(jnp.bfloat16)
    return (base + 0.5 * row_deltas.astype(jnp.float32)).astype(jnp.bfloat16)
```

```python
import functools

import numpy as np
import jax
import jax.numpy as jnp
from jax import lax
from jax.experimental import pallas as pl
from jax.experimental.pallas import tpu as pltpu
from jax.sharding import PartitionSpec as P

F32 = jnp.float32
BF16 = jnp.bfloat16
VMEM_BYTES = 56 * 2**20
SMALL = pl.CostEstimate(flops=1, bytes_accessed=1, transcendentals=0)


def params():
    return pltpu.CompilerParams(vmem_limit_bytes=VMEM_BYTES)


def line_plan(places):
    order = np.full((places, places), -1, np.int64)
    up = {}
    down = {}
    for z in range(places):
        rest = []
        for s in range(1, places):
            named = []
            if z <= s - 1:
                named.append((up, places - s + z))
            if z >= places - s:
                named.append((down, z - places + s))
            if len(named) == 2 and 2 * z >= places:
                named.reverse()
            for i, (table, chunk) in enumerate(named):
                if i == 0:
                    order[z, s - 1] = chunk
                    table[s, z] = s - 1
                else:
                    rest.append((table, s, chunk))
        order[z, places - 1] = z
        for table, s, chunk in rest:
            slot = int(np.flatnonzero(order[z] < 0)[0])
            assert slot < s
            order[z, slot] = chunk
            table[s, z] = slot
    return order, up, down


def pick(z, table, step, places, values):
    slots = sorted({table[step, p] for p in range(places) if (step, p) in table} & set(range(len(values))))
    result = values[slots[0]]
    for slot in slots[1:]:
        here = jnp.zeros((), jnp.bool_)
        for place in range(places):
            if table.get((step, place)) == slot:
                here = here | (z == place)
        result = jnp.where(here, values[slot], result)
    return result


def opening_body(scalars_ref, hidden_ref, scale_ref, w_ref, *refs):
    rest_ref, away_ref = refs[-2:]
    head = hidden_ref.shape[0] - rest_ref.shape[0]

    @pl.when(pl.program_id(0) == 0)
    def _():
        rest_ref[...] = (hidden_ref[head:].astype(F32) / scale_ref[...]).astype(BF16)

    away_ref[...] = jnp.dot(rest_ref[...], w_ref[...], preferred_element_type=F32).astype(BF16)


def opening(hidden, scale, weight, scalars, column, span, first, after=()):
    rows, depth = hidden.shape
    rest = rows - first
    tile = min(512, span)
    whole = lambda j, s: (0, 0)
    return pl.pallas_call(
        opening_body,
        out_shape=[
            jax.ShapeDtypeStruct((rest, depth), BF16),
            jax.ShapeDtypeStruct((rest, span), BF16),
        ],
        grid_spec=pltpu.PrefetchScalarGridSpec(
            num_scalar_prefetch=1,
            grid=(span // tile,),
            in_specs=[
                pl.BlockSpec((rows, depth), whole),
                pl.BlockSpec((1, depth), whole),
                pl.BlockSpec((depth, tile), lambda j, s: (0, s[column] * (span // tile) + j)),
            ]
            + [pl.BlockSpec(memory_space=pl.ANY)] * len(after),
            out_specs=[
                pl.BlockSpec((rest, depth), whole),
                pl.BlockSpec((rest, tile), lambda j, s: (0, j)),
            ],
        ),
        compiler_params=params(),
        cost_estimate=SMALL,
    )(scalars, hidden, scale.reshape(1, depth), weight, *after)


def product_body(added, scalars_ref, x_ref, w_ref, *refs):
    out_ref = refs[-1]
    total = jnp.dot(x_ref[...], w_ref[...], preferred_element_type=F32)
    for ref in refs[:added]:
        total = total + ref[...].astype(F32)
    out_ref[...] = total.astype(out_ref.dtype)


def sums_body(column, flagged, scalars_ref, sum_ref, *refs):
    got, others, outs = refs[:flagged], refs[flagged : 2 * flagged], refs[-flagged:]
    for i in range(flagged):
        mine = jnp.where(
            scalars_ref[column + 1 + i] != 0, sum_ref[...].astype(F32), others[i][...].astype(F32)
        )
        outs[i][...] = (mine + got[i][...].astype(F32)).astype(BF16)


def sum_body(scalars_ref, sum_ref, got_ref, *refs):
    refs[-1][...] = (sum_ref[...].astype(F32) + got_ref[...].astype(F32)).astype(BF16)


def sums(scalars, column, values, block, got, others=(), after=()):
    rows, width = got[0].shape
    tile = min(512, width)
    one = pl.BlockSpec((rows, tile), lambda j, s: (0, j))
    shape = jax.ShapeDtypeStruct((rows, width), BF16)
    count = len(others)
    return pl.pallas_call(
        functools.partial(sums_body, column, count) if count else sum_body,
        out_shape=[shape] * max(count, 1),
        grid_spec=pltpu.PrefetchScalarGridSpec(
            num_scalar_prefetch=1,
            grid=(width // tile,),
            in_specs=[pl.BlockSpec((rows, tile), lambda j, s: (block, j))]
            + [one] * (len(got) + count)
            + [pl.BlockSpec(memory_space=pl.ANY)] * len(after),
            out_specs=[one] * max(count, 1),
        ),
        compiler_params=params(),
        cost_estimate=SMALL,
    )(scalars, values, *got, *others, *after)


def merge_body(total_ref, got_ref, *refs):
    total_out, sent_out = refs[-2:]
    total = total_ref[...] + got_ref[...].astype(F32)
    total_out[...] = total
    sent_out[...] = total.astype(BF16)


def merge(total, got, after=()):
    block = pl.BlockSpec(total.shape, lambda: (0, 0))
    return pl.pallas_call(
        merge_body,
        out_shape=[jax.ShapeDtypeStruct(total.shape, F32), jax.ShapeDtypeStruct(total.shape, BF16)],
        in_specs=[block, block] + [pl.BlockSpec(memory_space=pl.ANY)] * len(after),
        out_specs=[block, block],
        compiler_params=params(),
        cost_estimate=SMALL,
    )(total, got, *after)


def product(x, weight, scalars, column, span, adds=(), after=(), dtype=BF16, rows=None, block=0, tile=512):
    depth = x.shape[1]
    rows = rows or x.shape[0]
    tile = min(tile, span)
    steps = span // tile
    out_block = pl.BlockSpec((rows, tile), lambda j, s: (0, j))
    size = jnp.dtype(dtype).itemsize
    out_shape = jax.ShapeDtypeStruct((rows, span), dtype)
    return pl.pallas_call(
        functools.partial(product_body, len(adds)),
        out_shape=out_shape,
        grid_spec=pltpu.PrefetchScalarGridSpec(
            num_scalar_prefetch=1,
            grid=(steps,),
            in_specs=[
                pl.BlockSpec((rows, depth), lambda j, s: (block, 0)),
                pl.BlockSpec((depth, tile), lambda j, s: (0, s[column] * steps + j)),
            ]
            + [
                out_block if a.shape[0] == rows else pl.BlockSpec((rows, tile), lambda j, s: (block, j))
                for a in adds
            ]
            + [pl.BlockSpec(memory_space=pl.ANY)] * len(after),
            out_specs=out_block,
        ),
        compiler_params=params(),
        cost_estimate=pl.CostEstimate(
            flops=2 * rows * depth * span,
            bytes_accessed=2 * rows * depth + 2 * depth * span + rows * span * (size + 2 * len(adds)),
            transcendentals=0,
        ),
    )(scalars, x, weight, *adds, *after)


def holds(slot, first, rank):
    lane = lax.broadcasted_iota(jnp.int32, slot.shape, 1)
    return slot == first + lane // rank


def by_half(own_ref, other_ref, use):
    j = pl.program_id(0)
    half = pl.num_programs(0) // 2

    @pl.when(j < half)
    def _():
        use(own_ref[...])

    @pl.when(j >= half)
    def _():
        use(other_ref[...])


def bank_specs(bank, tile):
    half = bank.shape[0] // tile
    return [
        pl.BlockSpec((tile, bank.shape[1]), lambda j: (jnp.minimum(j, half - 1), 0)),
        pl.BlockSpec((tile, bank.shape[1]), lambda j: (jnp.maximum(j - half, 0), 0)),
    ]


def shrink_body(rank, slot_ref, x_ref, own_ref, other_ref, *refs):
    out_ref, total = refs[-2:]
    j = pl.program_id(0)
    lanes = total.shape[1]
    each = own_ref.shape[0] // lanes

    @pl.when(j == 0)
    def _():
        total[...] = jnp.zeros_like(total)

    def use(bank):
        every = lax.dot_general(x_ref[...], bank, (((1,), (1,)), ((), ())), preferred_element_type=F32)
        slot = slot_ref[...]
        kept = total[...]
        for h in range(each):
            mine = holds(slot, (j * each + h) * (lanes // rank), rank)
            kept = kept + jnp.where(mine, every[:, h * lanes : (h + 1) * lanes], 0.0)
        total[...] = kept

    by_half(own_ref, other_ref, use)

    @pl.when(j == pl.num_programs(0) - 1)
    def _():
        both = total[...]
        both = both + pltpu.roll(both, rank, 1)
        half = out_ref.shape[0]
        left = lax.broadcasted_iota(jnp.int32, (half, lanes), 1) < rank
        out_ref[...] = jnp.where(left, both[:half], both[half:])


def shrink_rows(x, own, other, slot, rank, after=()):
    rows, depth = x.shape
    lanes = slot.shape[1]
    tile = min(4 * lanes, own.shape[0])
    return pl.pallas_call(
        functools.partial(shrink_body, rank),
        out_shape=jax.ShapeDtypeStruct((rows // 2, lanes), F32),
        grid=(2 * own.shape[0] // tile,),
        in_specs=[
            pl.BlockSpec((rows, lanes), lambda j: (0, 0)),
            pl.BlockSpec((rows, depth), lambda j: (0, 0)),
        ]
        + bank_specs(own, tile)
        + [pl.BlockSpec(memory_space=pl.ANY)] * len(after),
        out_specs=pl.BlockSpec((rows // 2, lanes), lambda j: (0, 0)),
        scratch_shapes=[pltpu.VMEM((rows, lanes), F32)],
        compiler_params=params(),
        cost_estimate=SMALL,
    )(slot, x, own, other, *after)


def expand_body(rank, slot_ref, shrunk_ref, own_ref, other_ref, rest_ref, *refs):
    out_ref, total, unpacked = refs[-3:]
    j = pl.program_id(0)
    lanes = shrunk_ref.shape[1]
    each = own_ref.shape[0] // lanes

    @pl.when(j == 0)
    def _():
        total[...] = jnp.zeros_like(total)
        packed = shrunk_ref[...].astype(F32)
        half = packed.shape[0]
        left = lax.broadcasted_iota(jnp.int32, packed.shape, 1) < rank
        turned = pltpu.roll(packed, rank, 1)
        unpacked[:half] = jnp.where(left, packed, turned)
        unpacked[half:] = jnp.where(left, turned, packed)

    def use(bank):
        slot = slot_ref[...]
        shrunk = unpacked[...]
        spread = [
            jnp.where(holds(slot, (j * each + h) * (lanes // rank), rank), shrunk, 0.0).astype(BF16)
            for h in range(each)
        ]
        total[...] += jnp.dot(jnp.concatenate(spread, axis=1), bank, preferred_element_type=F32)

    by_half(own_ref, other_ref, use)

    @pl.when(j == pl.num_programs(0) - 1)
    def _():
        delta = 0.5 * total[...].astype(BF16).astype(F32)
        head = delta.shape[0] - rest_ref.shape[0]
        out_ref[:head] = delta[:head]
        out_ref[head:] = rest_ref[...] + delta[head:]


def expand_rows(shrunk, own, other, slot, rank, rest, after=()):
    rows, lanes = slot.shape
    width = own.shape[1]
    tile = min(4 * lanes, own.shape[0])
    whole = lambda j: (0, 0)
    return pl.pallas_call(
        functools.partial(expand_body, rank),
        out_shape=jax.ShapeDtypeStruct((rows, width), F32),
        grid=(2 * own.shape[0] // tile,),
        in_specs=[pl.BlockSpec((rows, lanes), whole), pl.BlockSpec((rows // 2, lanes), whole)]
        + bank_specs(own, tile)
        + [pl.BlockSpec(rest.shape, whole)]
        + [pl.BlockSpec(memory_space=pl.ANY)] * len(after),
        out_specs=pl.BlockSpec((rows, width), whole),
        scratch_shapes=[pltpu.VMEM((rows, width), F32), pltpu.VMEM((rows, lanes), F32)],
        compiler_params=params(),
        cost_estimate=SMALL,
    )(slot, shrunk, own, other, rest, *after)


def finish_body(blocks, base_ref, kept_ref, part_ref, y_ref, *refs):
    ends, out_ref = refs[: 2 * blocks], refs[-1]
    size = ends[0].shape[0]
    head = base_ref.shape[0] - blocks * size
    total = base_ref[:head] + kept_ref[...].astype(F32) + part_ref[...].astype(F32)
    out_ref[:head] = total.astype(out_ref.dtype)
    for b in range(blocks):
        at = slice(head + b * size, head + (b + 1) * size)
        total = base_ref[at] + y_ref[b * size : (b + 1) * size].astype(F32)
        total = total + ends[2 * b][...].astype(F32) + ends[2 * b + 1][...].astype(F32)
        out_ref[at] = total.astype(out_ref.dtype)


def finish(base, kept, part, y_part, ends):
    rows, width = base.shape
    tile = min(width, 512)
    operands = [base, kept, part, y_part] + [end for pair in ends for end in pair]
    return pl.pallas_call(
        functools.partial(finish_body, len(ends)),
        out_shape=jax.ShapeDtypeStruct((rows, width), BF16),
        grid=(width // tile,),
        in_specs=[pl.BlockSpec((a.shape[0], tile), lambda j: (0, j)) for a in operands],
        out_specs=pl.BlockSpec((rows, tile), lambda j: (0, j)),
        compiler_params=params(),
        cost_estimate=SMALL,
    )(*operands)


def shards(
    hidden,
    channel_smooth_scale,
    weight,
    shrink_matrix_bank,
    expand_matrix_bank,
    row_adapter_index,
    adapter_storage_slot,
):
    rows, depth = hidden.shape
    tensors = lax.axis_size("tensor")
    assert lax.axis_size("owner") == 2 and tensors > 4 and tensors.bit_count() == 1
    places = tensors // 2
    width = weight.shape[1] // tensors
    adapters = adapter_storage_slot.shape[0]
    resident, rank, _ = shrink_matrix_bank.shape
    t = lax.axis_index("tensor")
    z, y = t // 2, t % 2
    o = lax.axis_index("owner")
    swap_y = [(i, i ^ 1) for i in range(tensors)]
    swap_owner = [(0, 1), (1, 0)]
    first = rows // 256 * 48
    lines = [list(range(i, tensors, 2)) for i in range(2)]
    order, up, down = line_plan(places)
    final = places - 1
    table = [
        [2 * order[i // 2, k] + 1 - i % 2 for k in range(places)]
        + [
            entry
            for k in range(places)
            for entry in (
                2 * order[i // 2, k] + i % 2,
                up.get((final, i // 2)) == final - 1,
                down.get((final, i // 2)) == final - 1,
            )
        ]
        + [0]
        for i in range(tensors)
    ]
    scalars = lax.dynamic_index_in_dim(jnp.asarray(np.array(table, np.int32)), t, keepdims=False)
    away_at = list(range(places))
    here_at = [places + 3 * k for k in range(places)]
    zero_at = 4 * places

    shrink = shrink_matrix_bank.reshape(resident * rank, depth)
    expand = expand_matrix_bank.reshape(resident * rank, width)
    shrink_other = lax.ppermute(shrink, "owner", swap_owner)
    expand_other = lax.ppermute(expand, "owner", swap_owner)
    names = lax.broadcasted_iota(jnp.int32, (1, adapters), 1)
    slot = jnp.sum(
        (row_adapter_index == names).astype(jnp.int32) * adapter_storage_slot[None, :], axis=1, keepdims=True
    )
    slot = jnp.where(slot < o * resident, slot + adapters, slot) - o * resident
    slot = jnp.broadcast_to(slot, (rows, 2 * rank))

    def send_along_y(k, last):
        sent = product(x_rest, weight, scalars, away_at[k], width, after=(last,))
        y_got.append(lax.ppermute(sent, "tensor", swap_y))
        return sent

    x_first = (hidden[:first].astype(F32) / channel_smooth_scale).astype(BF16)
    z_all = product(x_first, weight, scalars, zero_at, 2 * width * places, tile=2048)

    x_rest, away = opening(
        hidden, channel_smooth_scale, weight, scalars, away_at[0], width, first, after=(z_all,)
    )
    y_got = [lax.ppermute(away, "tensor", swap_y)]
    last = send_along_y(1, away)
    last = part_sum = shrink_rows(
        hidden, shrink, shrink_other, slot, rank, after=(last, expand_other)
    )
    z_sum = lax.psum_scatter(
        z_all, "tensor", scatter_dimension=1, axis_index_groups=lines, tiled=True
    )
    z_sent = jnp.where(y == 0, z_sum[:, width:], z_sum[:, :width])
    z_kept = jnp.where(y == 0, z_sum[:, :width], z_sum[:, width:])
    z_part = lax.ppermute(z_sent, "tensor", swap_y)
    every = lax.all_gather(part_sum, "tensor", axis=0)
    shrunk = jnp.sum(every, axis=0).astype(BF16)

    values = []
    arrived = ()
    for s in range(1, places):
        k = s - 1
        ups = [(a * 2 + i, a * 2 + 2 + i) for a in range(places - 1) for i in range(2) if a <= s - 1]
        downs = [(a * 2 + i, a * 2 - 2 + i) for a in range(1, places) for i in range(2) if a >= places - s]
        last = whole = product(
            x_rest, weight, scalars, here_at[k], width, (y_got[k],), after=(last,)
        )
        if s == 1:
            arrived = (lax.ppermute(last, "tensor", ups + downs),)
        else:
            if 2 * s <= places:
                if len(arrived) == 1:
                    last = whole = sums(scalars, 0, whole, 0, arrived, after=(last,))[0]
                else:
                    whole = whole.astype(F32) + arrived[0].astype(F32) + arrived[1].astype(F32)
                    whole = last = whole.astype(BF16)
                outs = whole, whole
            else:
                got = arrived if len(arrived) == 2 else arrived * 2
                if s < final:
                    outs = [
                        (pick(z, table, s, places, values + [whole]).astype(F32) + one.astype(F32)).astype(BF16)
                        for table, one in zip((up, down), got)
                    ]
                else:
                    others = [pick(z, table, s, places, values) for table in (up, down)]
                    outs = sums(scalars, here_at[k], whole, 0, got, others, after=(last,))
                last = outs[0]
            arrived = lax.ppermute(outs[0], "tensor", ups), lax.ppermute(outs[1], "tensor", downs)
        values.append(whole)
        if s + 1 < places:
            last = send_along_y(s + 1, last)
        if s == 1:
            last = own = product(
                x_rest, weight, scalars, here_at[final], width, after=(last,), dtype=F32
            )

    base = expand_rows(shrunk, expand, expand_other, slot, rank, own, after=(last,))
    return finish(base, z_kept, z_part, y_got[-1], [arrived])


def solution(mesh):
    placed = (
        P(("groups", "owner"), "tensor"),
        P("tensor"),
        P("tensor", None),
        P(("groups", "owner"), None, "tensor"),
        P(("groups", "owner"), None, "tensor"),
        P(("groups", "owner"), None),
        P("groups"),
    )
    return jax.shard_map(
        shards,
        mesh=mesh,
        in_specs=placed,
        out_specs=P(("groups", "owner"), "tensor"),
        check_vma=False,
    )
```

```python
import functools

import numpy as np
import jax
import jax.numpy as jnp
from jax import lax
from jax.experimental import pallas as pl
from jax.experimental.pallas import tpu as pltpu
from jax.sharding import PartitionSpec as P

F32 = jnp.float32
BF16 = jnp.bfloat16
SMALL = pl.CostEstimate(flops=1, bytes_accessed=1, transcendentals=0)


def params(large=False):
    return pltpu.CompilerParams(vmem_limit_bytes=(56 if large else 32) * 2**20)


def line_plan(places):
    order = np.full((places, places), -1, np.int64)
    up = {}
    down = {}
    for z in range(places):
        rest = []
        for s in range(1, places):
            named = []
            if z <= s - 1:
                named.append((up, places - s + z))
            if z >= places - s:
                named.append((down, z - places + s))
            if len(named) == 2 and 2 * z >= places:
                named.reverse()
            for i, (table, chunk) in enumerate(named):
                if i == 0:
                    order[z, s - 1] = chunk
                    table[s, z] = s - 1
                else:
                    rest.append((table, s, chunk))
        order[z, places - 1] = z
        for table, s, chunk in rest:
            slot = int(np.flatnonzero(order[z] < 0)[0])
            assert slot < s
            order[z, slot] = chunk
            table[s, z] = slot
    return order, up, down


def pick(z, table, step, places, values):
    slots = sorted({table[step, p] for p in range(places) if (step, p) in table} & set(range(len(values))))
    result = values[slots[0]]
    for slot in slots[1:]:
        here = jnp.zeros((), jnp.bool_)
        for place in range(places):
            if table.get((step, place)) == slot:
                here = here | (z == place)
        result = jnp.where(here, values[slot], result)
    return result


def opening_body(scalars_ref, hidden_ref, scale_ref, w_ref, x_ref, away_ref):
    @pl.when(pl.program_id(0) == 0)
    def _():
        x_ref[...] = (hidden_ref[...].astype(F32) / scale_ref[...]).astype(BF16)

    away_ref[...] = jnp.dot(x_ref[...], w_ref[...], preferred_element_type=F32).astype(BF16)


def opening(hidden, scale, weight, scalars, column, span):
    rows, depth = hidden.shape
    tile = min(512, span)
    whole = lambda j, s: (0, 0)
    return pl.pallas_call(
        opening_body,
        out_shape=[
            jax.ShapeDtypeStruct((rows, depth), BF16),
            jax.ShapeDtypeStruct((rows, span), BF16),
        ],
        grid_spec=pltpu.PrefetchScalarGridSpec(
            num_scalar_prefetch=1,
            grid=(span // tile,),
            in_specs=[
                pl.BlockSpec((rows, depth), whole),
                pl.BlockSpec((1, depth), whole),
                pl.BlockSpec((depth, tile), lambda j, s: (0, s[column] * (span // tile) + j)),
            ],
            out_specs=[
                pl.BlockSpec((rows, depth), whole),
                pl.BlockSpec((rows, tile), lambda j, s: (0, j)),
            ],
        ),
        compiler_params=params(True),
        cost_estimate=SMALL,
    )(scalars, hidden, scale.reshape(1, depth), weight)


def merge_body(total_ref, got_ref, *refs):
    total_out, sent_out = refs[-2:]
    total = total_ref[...] + got_ref[...].astype(F32)
    total_out[...] = total
    sent_out[...] = total.astype(BF16)


def merge(total, got, after=()):
    block = pl.BlockSpec(total.shape, lambda: (0, 0))
    return pl.pallas_call(
        merge_body,
        out_shape=[jax.ShapeDtypeStruct(total.shape, F32), jax.ShapeDtypeStruct(total.shape, BF16)],
        in_specs=[block, block] + [pl.BlockSpec(memory_space=pl.ANY)] * len(after),
        out_specs=[block, block],
        compiler_params=params(),
        cost_estimate=SMALL,
    )(total, got, *after)


def product_body(added, more, scalars_ref, x_ref, w_ref, *refs):
    out_ref = refs[-1]
    total = jnp.dot(x_ref[...], w_ref[...], preferred_element_type=F32)
    for ref in refs[:added]:
        total = total + ref[...].astype(F32)
    rows = x_ref.shape[0]
    out_ref[:rows] = total.astype(out_ref.dtype)
    if more:
        out_ref[rows:] = refs[added][...]


def sums_body(column, flagged, scalars_ref, sum_ref, *refs):
    got, others, outs = refs[:flagged], refs[flagged : 2 * flagged], refs[-flagged:]
    for i in range(flagged):
        mine = jnp.where(
            scalars_ref[column + 1 + i] != 0, sum_ref[...].astype(F32), others[i][...].astype(F32)
        )
        outs[i][...] = (mine + got[i][...].astype(F32)).astype(BF16)


def sum_body(scalars_ref, sum_ref, got_ref, *refs):
    refs[-1][...] = (sum_ref[...].astype(F32) + got_ref[...].astype(F32)).astype(BF16)


def sums(scalars, column, values, block, got, others=(), after=()):
    rows, width = got[0].shape
    tile = min(512, width)
    one = pl.BlockSpec((rows, tile), lambda j, s: (0, j))
    shape = jax.ShapeDtypeStruct((rows, width), BF16)
    count = len(others)
    return pl.pallas_call(
        functools.partial(sums_body, column, count) if count else sum_body,
        out_shape=[shape] * max(count, 1),
        grid_spec=pltpu.PrefetchScalarGridSpec(
            num_scalar_prefetch=1,
            grid=(width // tile,),
            in_specs=[pl.BlockSpec((rows, tile), lambda j, s: (block, j))]
            + [one] * (len(got) + count)
            + [pl.BlockSpec(memory_space=pl.ANY)] * len(after),
            out_specs=[one] * max(count, 1),
        ),
        compiler_params=params(),
        cost_estimate=SMALL,
    )(scalars, values, *got, *others, *after)


def merge_body(total_ref, got_ref, *refs):
    total_out, sent_out = refs[-2:]
    total = total_ref[...] + got_ref[...].astype(F32)
    total_out[...] = total
    sent_out[...] = total.astype(BF16)


def merge(total, got, after=()):
    block = pl.BlockSpec(total.shape, lambda: (0, 0))
    return pl.pallas_call(
        merge_body,
        out_shape=[jax.ShapeDtypeStruct(total.shape, F32), jax.ShapeDtypeStruct(total.shape, BF16)],
        in_specs=[block, block] + [pl.BlockSpec(memory_space=pl.ANY)] * len(after),
        out_specs=[block, block],
        compiler_params=params(),
        cost_estimate=SMALL,
    )(total, got, *after)


def product(x, weight, scalars, column, span, adds=(), after=(), dtype=BF16, rows=None, block=0, tile=512, tail=None, more=None):
    depth = x.shape[1]
    rows = rows or x.shape[0]
    tile = min(tile, span)
    steps = span // tile
    more = 0 if tail is None else more or tail.shape[0]
    out_block = pl.BlockSpec((rows + more, tile), lambda j, s: (0, j))
    block_in = pl.BlockSpec((rows, tile), lambda j, s: (0, j))
    tails = [] if tail is None else [tail]
    return pl.pallas_call(
        functools.partial(product_body, len(adds), more),
        out_shape=jax.ShapeDtypeStruct((rows + more, span), dtype),
        grid_spec=pltpu.PrefetchScalarGridSpec(
            num_scalar_prefetch=1,
            grid=(steps,),
            in_specs=[
                pl.BlockSpec((rows, depth), lambda j, s: (block, 0)),
                pl.BlockSpec((depth, tile), lambda j, s: (0, s[column] * steps + j)),
            ]
            + [
                block_in if a.shape[0] == rows else pl.BlockSpec((rows, tile), lambda j, s: (block, j))
                for a in adds
            ]
            + [pl.BlockSpec((more, tile), lambda j, s: (0, j)) for _ in tails]
            + [pl.BlockSpec(memory_space=pl.ANY)] * len(after),
            out_specs=out_block,
        ),
        compiler_params=params(True),
        cost_estimate=SMALL,
    )(scalars, x, weight, *adds, *tails, *after)


def holds(slot, first, rank):
    lane = lax.broadcasted_iota(jnp.int32, slot.shape, 1)
    return slot == first + lane // rank


def by_half(own_ref, other_ref, use):
    j = pl.program_id(0)
    half = pl.num_programs(0) // 2

    @pl.when(j < half)
    def _():
        use(own_ref[...])

    @pl.when(j >= half)
    def _():
        use(other_ref[...])


def bank_specs(bank, tile):
    half = bank.shape[0] // tile
    return [
        pl.BlockSpec((tile, bank.shape[1]), lambda j: (jnp.minimum(j, half - 1), 0)),
        pl.BlockSpec((tile, bank.shape[1]), lambda j: (jnp.maximum(j - half, 0), 0)),
    ]


def shrink_body(rank, slot_ref, x_ref, own_ref, other_ref, *refs):
    out_ref, total = refs[-2:]
    j = pl.program_id(0)
    lanes = total.shape[1]
    each = own_ref.shape[0] // lanes

    @pl.when(j == 0)
    def _():
        total[...] = jnp.zeros_like(total)

    def use(bank):
        every = lax.dot_general(x_ref[...], bank, (((1,), (1,)), ((), ())), preferred_element_type=F32)
        slot = slot_ref[...]
        kept = total[...]
        for h in range(each):
            mine = holds(slot, (j * each + h) * (lanes // rank), rank)
            kept = kept + jnp.where(mine, every[:, h * lanes : (h + 1) * lanes], 0.0)
        total[...] = kept

    by_half(own_ref, other_ref, use)

    @pl.when(j == pl.num_programs(0) - 1)
    def _():
        both = total[...]
        both = both + pltpu.roll(both, rank, 1)
        half = out_ref.shape[0]
        left = lax.broadcasted_iota(jnp.int32, (half, lanes), 1) < rank
        out_ref[...] = jnp.where(left, both[:half], both[half:])


def shrink_rows(x, own, other, slot, rank, after=()):
    rows, depth = x.shape
    lanes = slot.shape[1]
    tile = min(4 * lanes, own.shape[0])
    return pl.pallas_call(
        functools.partial(shrink_body, rank),
        out_shape=jax.ShapeDtypeStruct((rows // 2, lanes), F32),
        grid=(2 * own.shape[0] // tile,),
        in_specs=[
            pl.BlockSpec((rows, lanes), lambda j: (0, 0)),
            pl.BlockSpec((rows, depth), lambda j: (0, 0)),
        ]
        + bank_specs(own, tile)
        + [pl.BlockSpec(memory_space=pl.ANY)] * len(after),
        out_specs=pl.BlockSpec((rows // 2, lanes), lambda j: (0, 0)),
        scratch_shapes=[pltpu.VMEM((rows, lanes), F32)],
        compiler_params=params(),
        cost_estimate=SMALL,
    )(slot, x, own, other, *after)


def expand_body(rank, slot_ref, shrunk_ref, own_ref, other_ref, rest_ref, *refs):
    out_ref, total, unpacked = refs[-3:]
    j = pl.program_id(0)
    lanes = shrunk_ref.shape[1]
    each = own_ref.shape[0] // lanes

    @pl.when(j == 0)
    def _():
        total[...] = jnp.zeros_like(total)
        packed = shrunk_ref[...].astype(F32)
        half = packed.shape[0]
        left = lax.broadcasted_iota(jnp.int32, packed.shape, 1) < rank
        turned = pltpu.roll(packed, rank, 1)
        unpacked[:half] = jnp.where(left, packed, turned)
        unpacked[half:] = jnp.where(left, turned, packed)

    def use(bank):
        slot = slot_ref[...]
        shrunk = unpacked[...]
        spread = [
            jnp.where(holds(slot, (j * each + h) * (lanes // rank), rank), shrunk, 0.0).astype(BF16)
            for h in range(each)
        ]
        total[...] += jnp.dot(jnp.concatenate(spread, axis=1), bank, preferred_element_type=F32)

    by_half(own_ref, other_ref, use)

    @pl.when(j == pl.num_programs(0) - 1)
    def _():
        delta = 0.5 * total[...].astype(BF16).astype(F32)
        out_ref[...] = rest_ref[...] + delta


def expand_rows(shrunk, own, other, slot, rank, rest, after=()):
    rows, lanes = slot.shape
    width = own.shape[1]
    tile = min(4 * lanes, own.shape[0])
    whole = lambda j: (0, 0)
    return pl.pallas_call(
        functools.partial(expand_body, rank),
        out_shape=jax.ShapeDtypeStruct((rows, width), F32),
        grid=(2 * own.shape[0] // tile,),
        in_specs=[pl.BlockSpec((rows, lanes), whole), pl.BlockSpec((rows // 2, lanes), whole)]
        + bank_specs(own, tile)
        + [pl.BlockSpec(rest.shape, whole)]
        + [pl.BlockSpec(memory_space=pl.ANY)] * len(after),
        out_specs=pl.BlockSpec((rows, width), whole),
        scratch_shapes=[pltpu.VMEM((rows, width), F32), pltpu.VMEM((rows, lanes), F32)],
        compiler_params=params(),
        cost_estimate=SMALL,
    )(slot, shrunk, own, other, rest, *after)


def finish_body(blocks, base_ref, y_ref, *refs):
    ends, out_ref = refs[: 2 * blocks], refs[-1]
    size = ends[0].shape[0]
    for b in range(blocks):
        at = slice(b * size, (b + 1) * size)
        total = base_ref[at] + y_ref[at].astype(F32)
        total = total + ends[2 * b][...].astype(F32) + ends[2 * b + 1][...].astype(F32)
        out_ref[at] = total.astype(out_ref.dtype)


def finish(base, y_part, ends):
    rows, width = base.shape
    tile = min(width, 512)
    operands = [base, y_part] + [end for pair in ends for end in pair]
    return pl.pallas_call(
        functools.partial(finish_body, len(ends)),
        out_shape=jax.ShapeDtypeStruct((rows, width), BF16),
        grid=(width // tile,),
        in_specs=[pl.BlockSpec((a.shape[0], tile), lambda j: (0, j)) for a in operands],
        out_specs=pl.BlockSpec((rows, tile), lambda j: (0, j)),
        compiler_params=params(),
        cost_estimate=SMALL,
    )(*operands)


def shards(
    hidden,
    channel_smooth_scale,
    weight,
    shrink_matrix_bank,
    expand_matrix_bank,
    row_adapter_index,
    adapter_storage_slot,
):
    rows, depth = hidden.shape
    tensors = lax.axis_size("tensor")
    assert lax.axis_size("owner") == 2 and tensors > 4 and tensors.bit_count() == 1
    places = tensors // 2
    width = weight.shape[1] // tensors
    adapters = adapter_storage_slot.shape[0]
    resident, rank, _ = shrink_matrix_bank.shape
    t = lax.axis_index("tensor")
    z, y = t // 2, t % 2
    o = lax.axis_index("owner")
    swap_y = [(i, i ^ 1) for i in range(tensors)]
    swap_owner = [(0, 1), (1, 0)]
    blocks = 2
    part = rows // blocks
    order, up, down = line_plan(places)
    final = places - 1
    table = [
        [2 * order[i // 2, k] + 1 - i % 2 for k in range(places)]
        + [
            entry
            for k in range(places)
            for entry in (
                2 * order[i // 2, k] + i % 2,
                up.get((final, i // 2)) == final - 1,
                down.get((final, i // 2)) == final - 1,
            )
        ]
        for i in range(tensors)
    ]
    scalars = lax.dynamic_index_in_dim(jnp.asarray(np.array(table, np.int32)), t, keepdims=False)
    away_at = list(range(places))
    here_at = [places + 3 * k for k in range(places)]

    shrink = shrink_matrix_bank.reshape(resident * rank, depth)
    expand = expand_matrix_bank.reshape(resident * rank, width)
    shrink_other = lax.ppermute(shrink, "owner", swap_owner)
    expand_other = lax.ppermute(expand, "owner", swap_owner)
    names = lax.broadcasted_iota(jnp.int32, (1, adapters), 1)
    slot = jnp.sum(
        (row_adapter_index == names).astype(jnp.int32) * adapter_storage_slot[None, :], axis=1, keepdims=True
    )
    slot = jnp.where(slot < o * resident, slot + adapters, slot) - o * resident
    slot = jnp.broadcast_to(slot, (rows, 2 * rank))

    def there(k, last, tail=None):
        more = None
        if k == 1:
            tail, more = x, rows * rank // width + 16
        return product(x, weight, scalars, away_at[k], width, after=(last,), tail=tail, more=more)

    tails = {}

    def send_along_y(k, last):
        sent = there(k, last, tails.get(k))
        y_got.append(lax.ppermute(sent, "tensor", swap_y))
        return sent

    x, away = opening(hidden, channel_smooth_scale, weight, scalars, away_at[0], width)
    y_got = [lax.ppermute(away, "tensor", swap_y)]

    last = total = shrink_rows(hidden, shrink, shrink_other, slot, rank, after=(away, expand_other))
    sent = total.astype(BF16)
    for i in range(1, tensors.bit_length() - 1):
        pairs = [(j, j ^ 2**i) for j in range(tensors)]
        got = lax.ppermute(sent, "tensor", pairs)
        if i == 1:
            last = send_along_y(1, last)
        if i == 2:
            last = own = product(x, weight, scalars, here_at[final], width, after=(last,), dtype=F32)
        total, sent = merge(total, got, after=(last,))
        last = total
    tails[2] = sent.reshape(-1, width)

    values = []
    arrived = [()] * blocks
    for s in range(1, places):
        k = s - 1
        ups = [(a * 2 + i, a * 2 + 2 + i) for a in range(places - 1) for i in range(2) if a <= s - 1]
        downs = [(a * 2 + i, a * 2 - 2 + i) for a in range(1, places) for i in range(2) if a >= places - s]
        if s == 1:
            last = send_along_y(s + 1, last)
        parts = []
        if s > 1:
            last = whole = product(
                x, weight, scalars, here_at[k], width, (y_got[k],), after=(last,), dtype=F32
            )
        for b in range(blocks):
            if s == 1:
                last = product(
                    x, weight, scalars, here_at[k], width, (y_got[k],), after=(last,), rows=part, block=b
                )
                arrived[b] = (lax.ppermute(last, "tensor", ups + downs),)
                parts.append(last)
                continue
            cut = slice(b * part, (b + 1) * part)
            if 2 * s <= places:
                if len(arrived[b]) == 1:
                    last = sums(scalars, 0, whole, b, arrived[b], after=(last,))[0]
                else:
                    last = whole[cut].astype(F32) + arrived[b][0].astype(F32) + arrived[b][1].astype(F32)
                    last = last.astype(BF16)
                outs = last, last
                parts.append(last)
            else:
                got = arrived[b] if len(arrived[b]) == 2 else arrived[b] * 2
                earlier = [value[b] for value in values]
                if s < final:
                    parts.append(whole[cut])
                    outs = [
                        (pick(z, table, s, places, earlier + parts[-1:]).astype(F32) + one.astype(F32)).astype(BF16)
                        for table, one in zip((up, down), got)
                    ]
                else:
                    others = [pick(z, table, s, places, earlier) for table in (up, down)]
                    outs = sums(scalars, here_at[k], whole, b, got, others, after=(last,))
                last = outs[0]
            arrived[b] = lax.ppermute(outs[0], "tensor", ups), lax.ppermute(outs[1], "tensor", downs)
        values.append(parts)
        if 1 < s < final:
            last = send_along_y(s + 1, last)

    shrunk = (total + y_got[2][rows:].reshape(total.shape).astype(F32)).astype(BF16)
    base = expand_rows(shrunk, expand, expand_other, slot, rank, own, after=(last,))
    return finish(base, y_got[-1], arrived)


def solution(mesh):
    placed = (
        P(("groups", "owner"), "tensor"),
        P("tensor"),
        P("tensor", None),
        P(("groups", "owner"), None, "tensor"),
        P(("groups", "owner"), None, "tensor"),
        P(("groups", "owner"), None),
        P("groups"),
    )
    return jax.shard_map(
        shards,
        mesh=mesh,
        in_specs=placed,
        out_specs=P(("groups", "owner"), "tensor"),
        check_vma=False,
    )
```

```python
import functools

import numpy as np
import jax
import jax.numpy as jnp
from jax import lax
from jax.experimental import pallas as pl
from jax.experimental.pallas import tpu as pltpu
from jax.sharding import PartitionSpec as P

F32 = jnp.float32
BF16 = jnp.bfloat16
SMALL = pl.CostEstimate(flops=1, bytes_accessed=1, transcendentals=0)


def params(large=False):
    return pltpu.CompilerParams(vmem_limit_bytes=(56 if large else 48) * 2**20)


def line_plan(places):
    order = np.full((places, places), -1, np.int64)
    up = {}
    down = {}
    for z in range(places):
        rest = []
        for s in range(1, places):
            named = []
            if z <= s - 1:
                named.append((up, places - s + z))
            if z >= places - s:
                named.append((down, z - places + s))
            if len(named) == 2 and 2 * z >= places:
                named.reverse()
            for i, (table, chunk) in enumerate(named):
                if i == 0:
                    order[z, s - 1] = chunk
                    table[s, z] = s - 1
                else:
                    rest.append((table, s, chunk))
        order[z, places - 1] = z
        for table, s, chunk in rest:
            slot = int(np.flatnonzero(order[z] < 0)[0])
            assert slot < s
            order[z, slot] = chunk
            table[s, z] = slot
    return order, up, down


def pick(z, table, step, places, values):
    slots = sorted({table[step, p] for p in range(places) if (step, p) in table} & set(range(len(values))))
    result = values[slots[0]]
    for slot in slots[1:]:
        here = jnp.zeros((), jnp.bool_)
        for place in range(places):
            if table.get((step, place)) == slot:
                here = here | (z == place)
        result = jnp.where(here, values[slot], result)
    return result


def opening_body(scalars_ref, hidden_ref, scale_ref, w_ref, x_ref, away_ref):
    @pl.when(pl.program_id(0) == 0)
    def _():
        x_ref[...] = (hidden_ref[...].astype(F32) / scale_ref[...]).astype(BF16)

    away_ref[...] = jnp.dot(x_ref[...], w_ref[...], preferred_element_type=F32).astype(BF16)


def opening(hidden, scale, weight, scalars, column, span):
    rows, depth = hidden.shape
    tile = min(512, span)
    whole = lambda j, s: (0, 0)
    return pl.pallas_call(
        opening_body,
        out_shape=[
            jax.ShapeDtypeStruct((rows, depth), BF16),
            jax.ShapeDtypeStruct((rows, span), BF16),
        ],
        grid_spec=pltpu.PrefetchScalarGridSpec(
            num_scalar_prefetch=1,
            grid=(span // tile,),
            in_specs=[
                pl.BlockSpec((rows, depth), whole),
                pl.BlockSpec((1, depth), whole),
                pl.BlockSpec((depth, tile), lambda j, s: (0, s[column] * (span // tile) + j)),
            ],
            out_specs=[
                pl.BlockSpec((rows, depth), whole),
                pl.BlockSpec((rows, tile), lambda j, s: (0, j)),
            ],
        ),
        compiler_params=params(True),
        cost_estimate=SMALL,
    )(scalars, hidden, scale.reshape(1, depth), weight)


def merge_body(total_ref, got_ref, *refs):
    total_out, sent_out = refs[-2:]
    total = total_ref[...] + got_ref[...].astype(F32)
    total_out[...] = total
    sent_out[...] = total.astype(BF16)


def merge(total, got, after=()):
    block = pl.BlockSpec(total.shape, lambda: (0, 0))
    return pl.pallas_call(
        merge_body,
        out_shape=[jax.ShapeDtypeStruct(total.shape, F32), jax.ShapeDtypeStruct(total.shape, BF16)],
        in_specs=[block, block] + [pl.BlockSpec(memory_space=pl.ANY)] * len(after),
        out_specs=[block, block],
        compiler_params=params(),
        cost_estimate=SMALL,
    )(total, got, *after)


def product_body(added, more, scalars_ref, x_ref, w_ref, *refs):
    out_ref = refs[-1]
    total = jnp.dot(x_ref[...], w_ref[...], preferred_element_type=F32)
    for ref in refs[:added]:
        total = total + ref[...].astype(F32)
    rows = x_ref.shape[0]
    out_ref[:rows] = total.astype(out_ref.dtype)
    if more:
        out_ref[rows:] = refs[added][...]


def sums_body(column, flagged, scalars_ref, sum_ref, *refs):
    got, others, outs = refs[:flagged], refs[flagged : 2 * flagged], refs[-flagged:]
    for i in range(flagged):
        mine = jnp.where(
            scalars_ref[column + 1 + i] != 0, sum_ref[...].astype(F32), others[i][...].astype(F32)
        )
        outs[i][...] = (mine + got[i][...].astype(F32)).astype(BF16)


def sum_body(scalars_ref, sum_ref, got_ref, *refs):
    refs[-1][...] = (sum_ref[...].astype(F32) + got_ref[...].astype(F32)).astype(BF16)


def sums(scalars, column, values, block, got, others=(), after=()):
    rows, width = got[0].shape
    tile = min(512, width)
    one = pl.BlockSpec((rows, tile), lambda j, s: (0, j))
    shape = jax.ShapeDtypeStruct((rows, width), BF16)
    count = len(others)
    return pl.pallas_call(
        functools.partial(sums_body, column, count) if count else sum_body,
        out_shape=[shape] * max(count, 1),
        grid_spec=pltpu.PrefetchScalarGridSpec(
            num_scalar_prefetch=1,
            grid=(width // tile,),
            in_specs=[pl.BlockSpec((rows, tile), lambda j, s: (block, j))]
            + [one] * (len(got) + count)
            + [pl.BlockSpec(memory_space=pl.ANY)] * len(after),
            out_specs=[one] * max(count, 1),
        ),
        compiler_params=params(),
        cost_estimate=SMALL,
    )(scalars, values, *got, *others, *after)


def merge_body(total_ref, got_ref, *refs):
    total_out, sent_out = refs[-2:]
    total = total_ref[...] + got_ref[...].astype(F32)
    total_out[...] = total
    sent_out[...] = total.astype(BF16)


def merge(total, got, after=()):
    block = pl.BlockSpec(total.shape, lambda: (0, 0))
    return pl.pallas_call(
        merge_body,
        out_shape=[jax.ShapeDtypeStruct(total.shape, F32), jax.ShapeDtypeStruct(total.shape, BF16)],
        in_specs=[block, block] + [pl.BlockSpec(memory_space=pl.ANY)] * len(after),
        out_specs=[block, block],
        compiler_params=params(),
        cost_estimate=SMALL,
    )(total, got, *after)


def product(x, weight, scalars, column, span, adds=(), after=(), dtype=BF16, rows=None, block=0, tile=512, tail=None, more=None):
    depth = x.shape[1]
    rows = rows or x.shape[0]
    tile = min(tile, span)
    steps = span // tile
    more = 0 if tail is None else more or tail.shape[0]
    out_block = pl.BlockSpec((rows + more, tile), lambda j, s: (0, j))
    block_in = pl.BlockSpec((rows, tile), lambda j, s: (0, j))
    tails = [] if tail is None else [tail]
    return pl.pallas_call(
        functools.partial(product_body, len(adds), more),
        out_shape=jax.ShapeDtypeStruct((rows + more, span), dtype),
        grid_spec=pltpu.PrefetchScalarGridSpec(
            num_scalar_prefetch=1,
            grid=(steps,),
            in_specs=[
                pl.BlockSpec((rows, depth), lambda j, s: (block, 0)),
                pl.BlockSpec((depth, tile), lambda j, s: (0, s[column] * steps + j)),
            ]
            + [
                block_in if a.shape[0] == rows else pl.BlockSpec((rows, tile), lambda j, s: (block, j))
                for a in adds
            ]
            + [pl.BlockSpec((more, tile), lambda j, s: (0, j)) for _ in tails]
            + [pl.BlockSpec(memory_space=pl.ANY)] * len(after),
            out_specs=out_block,
        ),
        compiler_params=params(True),
        cost_estimate=SMALL,
    )(scalars, x, weight, *adds, *tails, *after)


def holds(slot, first, rank):
    lane = lax.broadcasted_iota(jnp.int32, slot.shape, 1)
    return slot == first + lane // rank


def by_half(own_ref, other_ref, use):
    j = pl.program_id(0)
    half = pl.num_programs(0) // 2

    @pl.when(j < half)
    def _():
        use(own_ref[...])

    @pl.when(j >= half)
    def _():
        use(other_ref[...])


def bank_specs(bank, tile):
    half = bank.shape[0] // tile
    return [
        pl.BlockSpec((tile, bank.shape[1]), lambda j: (jnp.minimum(j, half - 1), 0)),
        pl.BlockSpec((tile, bank.shape[1]), lambda j: (jnp.maximum(j - half, 0), 0)),
    ]


def rows_body(added, *refs):
    total = refs[0][...].astype(F32)
    for ref in refs[1:added]:
        total = total + ref[...].astype(F32)
    refs[-1][...] = total


def cut_spec(array, rows, tile, block):
    if array.shape[0] == rows:
        return pl.BlockSpec((rows, tile), lambda j, *s: (0, j))
    return pl.BlockSpec((rows, tile), lambda j, *s: (block, j))


def add_rows(values, rows, block, after=()):
    width = values[0].shape[1]
    tile = min(512, width)
    return pl.pallas_call(
        functools.partial(rows_body, len(values)),
        out_shape=jax.ShapeDtypeStruct((rows, width), F32),
        grid=(width // tile,),
        in_specs=[cut_spec(v, rows, tile, block) for v in values]
        + [pl.BlockSpec(memory_space=pl.ANY)] * len(after),
        out_specs=pl.BlockSpec((rows, tile), lambda j: (0, j)),
        compiler_params=params(),
        cost_estimate=SMALL,
    )(*values, *after)


def shrink_body(rank, slot_ref, x_ref, own_ref, other_ref, *refs):
    out_ref, total = refs[-2:]
    j = pl.program_id(0)
    lanes = total.shape[1]
    each = own_ref.shape[0] // lanes

    @pl.when(j == 0)
    def _():
        total[...] = jnp.zeros_like(total)

    def use(bank):
        every = lax.dot_general(x_ref[...], bank, (((1,), (1,)), ((), ())), preferred_element_type=F32)
        slot = slot_ref[...]
        kept = total[...]
        for h in range(each):
            mine = holds(slot, (j * each + h) * (lanes // rank), rank)
            kept = kept + jnp.where(mine, every[:, h * lanes : (h + 1) * lanes], 0.0)
        total[...] = kept

    by_half(own_ref, other_ref, use)

    @pl.when(j == pl.num_programs(0) - 1)
    def _():
        both = total[...]
        both = both + pltpu.roll(both, rank, 1)
        half = out_ref.shape[0]
        left = lax.broadcasted_iota(jnp.int32, (half, lanes), 1) < rank
        out_ref[...] = jnp.where(left, both[:half], both[half:])


def shrink_rows(x, own, other, slot, rank, after=()):
    rows, depth = x.shape
    lanes = slot.shape[1]
    tile = min(4 * lanes, own.shape[0])
    return pl.pallas_call(
        functools.partial(shrink_body, rank),
        out_shape=jax.ShapeDtypeStruct((rows // 2, lanes), F32),
        grid=(2 * own.shape[0] // tile,),
        in_specs=[
            pl.BlockSpec((rows, lanes), lambda j: (0, 0)),
            pl.BlockSpec((rows, depth), lambda j: (0, 0)),
        ]
        + bank_specs(own, tile)
        + [pl.BlockSpec(memory_space=pl.ANY)] * len(after),
        out_specs=pl.BlockSpec((rows // 2, lanes), lambda j: (0, 0)),
        scratch_shapes=[pltpu.VMEM((rows, lanes), F32)],
        compiler_params=params(),
        cost_estimate=SMALL,
    )(slot, x, own, other, *after)


def expand_body(rank, slot_ref, shrunk_ref, own_ref, other_ref, rest_ref, *refs):
    out_ref, total, unpacked = refs[-3:]
    j = pl.program_id(0)
    lanes = shrunk_ref.shape[1]
    each = own_ref.shape[0] // lanes

    @pl.when(j == 0)
    def _():
        total[...] = jnp.zeros_like(total)
        packed = shrunk_ref[...].astype(F32)
        half = packed.shape[0]
        left = lax.broadcasted_iota(jnp.int32, packed.shape, 1) < rank
        turned = pltpu.roll(packed, rank, 1)
        unpacked[:half] = jnp.where(left, packed, turned)
        unpacked[half:] = jnp.where(left, turned, packed)

    def use(bank):
        slot = slot_ref[...]
        shrunk = unpacked[...]
        spread = [
            jnp.where(holds(slot, (j * each + h) * (lanes // rank), rank), shrunk, 0.0).astype(BF16)
            for h in range(each)
        ]
        total[...] += jnp.dot(jnp.concatenate(spread, axis=1), bank, preferred_element_type=F32)

    by_half(own_ref, other_ref, use)

    @pl.when(j == pl.num_programs(0) - 1)
    def _():
        delta = 0.5 * total[...].astype(BF16).astype(F32)
        out_ref[...] = rest_ref[...] + delta


def expand_rows(shrunk, own, other, slot, rank, rest, after=()):
    rows, lanes = slot.shape
    width = own.shape[1]
    tile = min(4 * lanes, own.shape[0])
    whole = lambda j: (0, 0)
    return pl.pallas_call(
        functools.partial(expand_body, rank),
        out_shape=jax.ShapeDtypeStruct((rows, width), F32),
        grid=(2 * own.shape[0] // tile,),
        in_specs=[pl.BlockSpec((rows, lanes), whole), pl.BlockSpec((rows // 2, lanes), whole)]
        + bank_specs(own, tile)
        + [pl.BlockSpec(rest.shape, whole)]
        + [pl.BlockSpec(memory_space=pl.ANY)] * len(after),
        out_specs=pl.BlockSpec((rows, width), whole),
        scratch_shapes=[pltpu.VMEM((rows, width), F32), pltpu.VMEM((rows, lanes), F32)],
        compiler_params=params(),
        cost_estimate=SMALL,
    )(slot, shrunk, own, other, rest, *after)


def finish_body(blocks, base_ref, y_ref, *refs):
    ends, out_ref = refs[: 2 * blocks], refs[-1]
    size = ends[0].shape[0]
    for b in range(blocks):
        at = slice(b * size, (b + 1) * size)
        total = base_ref[at] + y_ref[at].astype(F32)
        total = total + ends[2 * b][...].astype(F32) + ends[2 * b + 1][...].astype(F32)
        out_ref[at] = total.astype(out_ref.dtype)


def finish(base, y_part, ends):
    rows, width = base.shape
    tile = min(width, 512)
    operands = [base, y_part] + [end for pair in ends for end in pair]
    return pl.pallas_call(
        functools.partial(finish_body, len(ends)),
        out_shape=jax.ShapeDtypeStruct((rows, width), BF16),
        grid=(width // tile,),
        in_specs=[pl.BlockSpec((a.shape[0], tile), lambda j: (0, j)) for a in operands],
        out_specs=pl.BlockSpec((rows, tile), lambda j: (0, j)),
        compiler_params=params(),
        cost_estimate=SMALL,
    )(*operands)


def shards(
    hidden,
    channel_smooth_scale,
    weight,
    shrink_matrix_bank,
    expand_matrix_bank,
    row_adapter_index,
    adapter_storage_slot,
):
    rows, depth = hidden.shape
    tensors = lax.axis_size("tensor")
    assert lax.axis_size("owner") == 2 and tensors > 4 and tensors.bit_count() == 1
    places = tensors // 2
    width = weight.shape[1] // tensors
    adapters = adapter_storage_slot.shape[0]
    resident, rank, _ = shrink_matrix_bank.shape
    t = lax.axis_index("tensor")
    z, y = t // 2, t % 2
    o = lax.axis_index("owner")
    swap_y = [(i, i ^ 1) for i in range(tensors)]
    swap_owner = [(0, 1), (1, 0)]
    blocks = 2
    part = rows // blocks
    order, up, down = line_plan(places)
    final = places - 1
    table = [
        [2 * order[i // 2, k] + 1 - i % 2 for k in range(places)]
        + [
            entry
            for k in range(places)
            for entry in (
                2 * order[i // 2, k] + i % 2,
                up.get((final, i // 2)) == final - 1,
                down.get((final, i // 2)) == final - 1,
            )
        ]
        for i in range(tensors)
    ]
    scalars = lax.dynamic_index_in_dim(jnp.asarray(np.array(table, np.int32)), t, keepdims=False)
    away_at = list(range(places))
    here_at = [places + 3 * k for k in range(places)]

    shrink = shrink_matrix_bank.reshape(resident * rank, depth)
    expand = expand_matrix_bank.reshape(resident * rank, width)
    shrink_other = lax.ppermute(shrink, "owner", swap_owner)
    expand_other = lax.ppermute(expand, "owner", swap_owner)
    names = lax.broadcasted_iota(jnp.int32, (1, adapters), 1)
    slot = jnp.sum(
        (row_adapter_index == names).astype(jnp.int32) * adapter_storage_slot[None, :], axis=1, keepdims=True
    )
    slot = jnp.where(slot < o * resident, slot + adapters, slot) - o * resident
    slot = jnp.broadcast_to(slot, (rows, 2 * rank))

    def there(k, last, tail=None):
        more = None
        if k == 1:
            tail, more = x, rows * rank // width + 16
        return product(x, weight, scalars, away_at[k], width, after=(last,), tail=tail, more=more)

    tails = {}

    def send_along_y(k, last):
        sent = there(k, last, tails.get(k))
        y_got.append(lax.ppermute(sent, "tensor", swap_y))
        return sent

    x, away = opening(hidden, channel_smooth_scale, weight, scalars, away_at[0], width)
    y_got = [lax.ppermute(away, "tensor", swap_y)]

    last = total = shrink_rows(hidden, shrink, shrink_other, slot, rank, after=(away, expand_other))
    sent = total.astype(BF16)
    for i in range(1, tensors.bit_length() - 1):
        pairs = [(j, j ^ 2**i) for j in range(tensors)]
        got = lax.ppermute(sent, "tensor", pairs)
        if i == 1:
            last = send_along_y(1, last)
        if i == 2:
            last = own = product(x, weight, scalars, here_at[final], width, after=(last,), dtype=F32)
        total, sent = merge(total, got, after=(last,))
        last = total
    tails[2] = sent.reshape(-1, width)

    values = []
    arrived = [()] * blocks
    for s in range(1, places):
        k = s - 1
        ups = [(a * 2 + i, a * 2 + 2 + i) for a in range(places - 1) for i in range(2) if a <= s - 1]
        downs = [(a * 2 + i, a * 2 - 2 + i) for a in range(1, places) for i in range(2) if a >= places - s]
        if s == 1:
            last = send_along_y(s + 1, last)
        parts = []
        if s > 1:
            last = whole = add_rows((mine, y_got[k]), rows, 0, after=(last,))
        for b in range(blocks):
            if s == 1:
                last = product(
                    x, weight, scalars, here_at[k], width, (y_got[k],), after=(last,), rows=part, block=b
                )
                arrived[b] = (lax.ppermute(last, "tensor", ups + downs),)
                parts.append(last)
                continue
            cut = slice(b * part, (b + 1) * part)
            if 2 * s <= places:
                if len(arrived[b]) == 1:
                    last = sums(scalars, 0, whole, b, arrived[b], after=(last,))[0]
                else:
                    last = whole[cut].astype(F32) + arrived[b][0].astype(F32) + arrived[b][1].astype(F32)
                    last = last.astype(BF16)
                outs = last, last
                parts.append(last)
            else:
                got = arrived[b] if len(arrived[b]) == 2 else arrived[b] * 2
                earlier = [value[b] for value in values]
                if s < final:
                    parts.append(whole[cut])
                    outs = [
                        (pick(z, table, s, places, earlier + parts[-1:]).astype(F32) + one.astype(F32)).astype(BF16)
                        for table, one in zip((up, down), got)
                    ]
                else:
                    others = [pick(z, table, s, places, earlier) for table in (up, down)]
                    outs = sums(scalars, here_at[k], whole, b, got, others, after=(last,))
                last = outs[0]
            arrived[b] = lax.ppermute(outs[0], "tensor", ups), lax.ppermute(outs[1], "tensor", downs)
        values.append(parts)
        if s < final:
            last = mine = product(x, weight, scalars, here_at[s], width, after=(last,), dtype=F32)
        if 1 < s < final:
            last = send_along_y(s + 1, last)

    shrunk = (total + y_got[2][rows:].reshape(total.shape).astype(F32)).astype(BF16)
    base = expand_rows(shrunk, expand, expand_other, slot, rank, own, after=(last,))
    return finish(base, y_got[-1], arrived)


def solution(mesh):
    placed = (
        P(("groups", "owner"), "tensor"),
        P("tensor"),
        P("tensor", None),
        P(("groups", "owner"), None, "tensor"),
        P(("groups", "owner"), None, "tensor"),
        P(("groups", "owner"), None),
        P("groups"),
    )
    return jax.shard_map(
        shards,
        mesh=mesh,
        in_specs=placed,
        out_specs=P(("groups", "owner"), "tensor"),
        check_vma=False,
    )
```
